512 devices in a mesh: row: 16 (over y, core), col: 4 (over z_hi), height: 8 (over x, z_lo).
Axes of the slice: x: 4, y: 8, z: 8 (z_hi: 4, z_lo: 2; z = z_hi * 2 + z_lo), core: 2. Of those that a mesh axis runs over, the one named last changes fastest.
Arguments:
- impedance: bfloat16 [16, 4, 8, 1536, 1536], P('row', 'col', 'height'), may hold values from -0.125 to 0.125
- sources: bfloat16 [16, 4, 8, 48, 1536], P('row', 'col', 'height'), may hold values from -6 to 6
- coupling: int32 [16, 4, 8, 6], P('row', 'col', 'height'), may hold values 0 or 1
Outputs:
- outgoing: bfloat16 [16, 4, 8, 48, 1536], P('row', 'col', 'height')
The draws below stay inside these ranges and needn't reach their ends.
Inputs may be any that keep to these rules, and one draw needn't show every extreme that they name: `coupling`: 1 marks a coupled face, 0 an absorbing one.
All inputs are finite; a program needn't handle non-finite values. No bound on the sum of `coupling` on one device may be relied on, other than what follows from the above.
Results may differ from the reference program's by a relative error of at most 0.014.
Values may be sent and summed in bfloat16 or wider, within the bound.
A program may use at most 64 MiB of HBM per device.

```python
import jax
import jax.numpy as jnp
from jax import lax

FACE = 256
ORDER = 1536
EXC = 48
ITERS = 8
BRICK_ROWS = 16
BRICK_COLS = 4
BRICK_LEVELS = 8


def with_ends(drawn, stream_key, low, high):
    extent = drawn.shape
    index_at = [jax.random.randint(jax.random.fold_in(stream_key, axis), (), 0, extent[axis]) for axis in range(len(extent))]
    drawn = drawn.at[tuple(index_at)].set(low)
    longest = extent.index(max(extent))
    index_at[longest] = (index_at[longest] + 1) % extent[longest]
    return drawn.at[tuple(index_at)].set(high)


def level_of(key, extent, split, smallest, high):
    def one(axis_at, shards_of):
        steps = jax.random.uniform(jax.random.fold_in(jax.random.fold_in(key, 6), axis_at), (shards_of,), jnp.float32, smallest / len(split), high / len(split))
        return jnp.repeat(jnp.exp(steps), extent[axis_at] // shards_of).reshape((-1,) + (1,) * (len(extent) - axis_at - 1))

    gain = one(*split[0])
    for cut in split[1:]:
        gain = gain * one(*cut)
    return gain


def bell_draw(stream_key, dims, deviation, most, pieces=(), held_as=jnp.bfloat16):
    array = deviation * jax.random.normal(stream_key, dims, jnp.float32)
    if pieces:
        array = array * level_of(stream_key, dims, pieces, -0.22, 0.18)
    return jnp.clip(array, -most, most).astype(held_as)


def setup_inputs(seed: int = 0) -> dict:
    splits = jax.random.split(jax.random.key(seed), 4)
    impedance = bell_draw(splits[0], (BRICK_ROWS, BRICK_COLS, BRICK_LEVELS, ORDER, ORDER), (3 * ORDER // 2) ** -0.5, 0.125, ((0, 16), (1, 4), (2, 8)))
    sources = bell_draw(splits[1], (BRICK_ROWS, BRICK_COLS, BRICK_LEVELS, EXC, ORDER), 1.0, 6.0, ((0, 16), (1, 4), (2, 8)))
    coupling = with_ends((jax.random.randint(splits[2], (BRICK_ROWS, BRICK_COLS, BRICK_LEVELS, 6), 0, 4) < 3).astype(jnp.int32), jax.random.fold_in(splits[2], 1), 0, 1)
    return {"impedance": impedance, "sources": sources, "coupling": coupling}


def shifted(fields, axis_pos):
    low_face = fields[:, :, :, :, 2 * axis_pos, :]
    high_face = fields[:, :, :, :, 2 * axis_pos + 1, :]
    length = high_face.shape[axis_pos]
    empty = jnp.zeros_like(lax.slice_in_dim(high_face, 0, 1, axis=axis_pos))
    from_below = jnp.concatenate([empty, lax.slice_in_dim(high_face, 0, length - 1, axis=axis_pos)], axis=axis_pos)
    from_above = jnp.concatenate([lax.slice_in_dim(low_face, 1, length, axis=axis_pos), empty], axis=axis_pos)
    return from_below, from_above


def apply_one(pair):
    driven_brick, map_brick = pair
    product = jnp.dot(driven_brick.astype(jnp.float32), map_brick.astype(jnp.float32), precision=lax.Precision.HIGHEST)
    return product.astype(jnp.bfloat16)


def reference(impedance, sources, coupling):
    bricks = BRICK_ROWS * BRICK_COLS * BRICK_LEVELS
    flat_maps = impedance.reshape(bricks, ORDER, ORDER)
    couple_gain = coupling.astype(jnp.float32)[:, :, :, None, :, None]
    incoming = jnp.zeros(sources.shape, jnp.bfloat16)
    outgoing = incoming
    for iteration in range(ITERS):
        driven = (incoming.astype(jnp.float32) + sources.astype(jnp.float32)).astype(jnp.bfloat16)
        outgoing = lax.map(apply_one, (driven.reshape(bricks, EXC, ORDER), flat_maps)).reshape(sources.shape)
        if iteration + 1 < ITERS:
            fields = outgoing.reshape(BRICK_ROWS, BRICK_COLS, BRICK_LEVELS, EXC, 6, FACE)
            collected = []
            for axis_pos in range(3):
                from_below, from_above = shifted(fields, axis_pos)
                collected.append(from_below)
                collected.append(from_above)
            stacked = jnp.stack(collected, axis=4).astype(jnp.float32) * couple_gain
            incoming = stacked.astype(jnp.bfloat16).reshape(sources.shape)
    return outgoing
```

```python
import functools

import jax
import jax.numpy as jnp
from jax import lax
from jax.experimental import pallas as pl
from jax.experimental.pallas import tpu as pltpu
from jax.sharding import PartitionSpec as P

ITERS = 8
FACES = 6
AXES = ("row", "col", "height")
MESH = pl.DeviceIdType.MESH
GROUPS = ((0, 32), (32, 16))
STAGES = ((0, 1), (4, 5), (2, 3))
SEND_ORDER = (2, 3, 4, 5, 0, 1)


def kernel(sizes, face, z_hbm, src_hbm, gain_ref, out,
           z, src, driven, acc, send, recv, z_sem, src_sem, send_sem, recv_sem):
    pos = [lax.axis_index(name) for name in AXES]

    def neighbour(f):
        axis, up = f // 2, f % 2
        n = sizes[axis]
        ids = list(pos)
        ids[axis] = lax.rem(pos[axis] + (1 if up else n - 1), n)
        return tuple(ids)

    targets = [neighbour(f) for f in range(FACES)]
    exists = [
        pos[f // 2] < sizes[f // 2] - 1 if f % 2 else pos[f // 2] > 0 for f in range(FACES)
    ]

    def z_copy(f):
        return pltpu.make_async_copy(z_hbm.at[:, f * face:(f + 1) * face], z.at[f], z_sem.at[f])

    src_copy = pltpu.make_async_copy(src_hbm, src, src_sem)
    src_copy.start()
    for f in SEND_ORDER:
        z_copy(f).start()
    barrier = pltpu.get_barrier_semaphore()
    for f in range(FACES):

        @pl.when(exists[f])
        def _():
            pl.semaphore_signal(barrier, inc=1, device_id=targets[f], device_id_type=MESH)

        @pl.when(jnp.logical_not(exists[f]))
        def _():
            for slot in range(ITERS - 1):
                recv[slot, f] = jnp.zeros(recv.shape[2:], recv.dtype)

    gains = [gain_ref[f].astype(jnp.float32) for f in range(FACES)]

    def remote(slot, f, g):
        lo, rows = GROUPS[g]
        return pltpu.make_async_remote_copy(
            src_ref=send.at[slot, f, lo:lo + rows],
            dst_ref=recv.at[slot, f ^ 1, lo:lo + rows],
            send_sem=send_sem.at[slot, f, g],
            recv_sem=recv_sem.at[slot, f ^ 1, g],
            device_id=targets[f],
            device_id_type=MESH,
        )

    def arrival(slot, f, g):
        return remote(slot, f ^ 1, g)

    def emit(slot, f, g, value):
        lo, rows = GROUPS[g]
        send[slot, f, lo:lo + rows] = value.astype(jnp.bfloat16)

        @pl.when(exists[f])
        def _():
            remote(slot, f, g).start()

    src_copy.wait()
    for i, f in enumerate(SEND_ORDER):
        z_copy(f).wait()
        value = jnp.dot(src[...], z[f], preferred_element_type=jnp.float32)
        if i == 0:
            pl.semaphore_wait(barrier, sum(here.astype(jnp.int32) for here in exists))
        for g, (lo, rows) in enumerate(GROUPS):
            emit(0, f, g, value[lo:lo + rows])

    def accept(slot, g, finish):
        lo, rows = GROUPS[g]
        for s, faces in enumerate(STAGES):
            for f in faces:

                @pl.when(exists[f])
                def _():
                    arrival(slot, f, g).wait_recv()

                cols = slice(f * face, (f + 1) * face)
                driven[lo:lo + rows, cols] = (
                    recv[slot, f, lo:lo + rows].astype(jnp.float32) * gains[f]
                    + src[lo:lo + rows, cols].astype(jnp.float32)
                ).astype(jnp.bfloat16)
            k0, k1 = faces[0] * face, (faces[-1] + 1) * face
            for f in SEND_ORDER:
                part = jnp.dot(driven[lo:lo + rows, k0:k1], z[f, k0:k1], preferred_element_type=jnp.float32)
                if s > 0:
                    part = acc[f, lo:lo + rows] + part
                if s + 1 < len(STAGES):
                    acc[f, lo:lo + rows] = part
                else:
                    finish(f, part)

    def step(iteration, carry):
        for g in range(len(GROUPS)):
            accept(iteration - 1, g, lambda f, value: emit(iteration, f, g, value))
        for g in range(len(GROUPS)):
            for f in range(FACES):

                @pl.when(exists[f])
                def _():
                    remote(iteration - 1, f, g).wait_send()

        return carry

    lax.fori_loop(1, ITERS - 1, step, 0)

    def finish_last(g):
        lo, rows = GROUPS[g]

        def finish(f, value):
            out[lo:lo + rows, f * face:(f + 1) * face] = value.astype(jnp.bfloat16)

        return finish

    for g in range(len(GROUPS)):
        accept(ITERS - 2, g, finish_last(g))
    for g in range(len(GROUPS)):
        for f in range(FACES):

            @pl.when(exists[f])
            def _():
                remote(ITERS - 2, f, g).wait_send()


def solution(mesh):
    sizes = tuple(mesh.shape[name] for name in AXES)

    def shards(impedance, sources, coupling):
        square = impedance[0, 0, 0]
        excite = sources[0, 0, 0]
        gain = coupling[0, 0, 0]
        exc, order = excite.shape
        face = order // FACES
        groups = len(GROUPS)
        slots = ITERS - 1
        outgoing = pl.pallas_call(
            functools.partial(kernel, sizes, face),
            out_shape=pltpu.VMEM((exc, order), jnp.bfloat16),
            in_specs=[
                pl.BlockSpec(memory_space=pl.ANY),
                pl.BlockSpec(memory_space=pl.ANY),
                pl.BlockSpec(memory_space=pltpu.SMEM),
            ],
            out_specs=pl.BlockSpec(memory_space=pltpu.VMEM),
            scratch_shapes=[
                pltpu.VMEM((FACES, order, face), jnp.bfloat16),
                pltpu.VMEM((exc, order), jnp.bfloat16),
                pltpu.VMEM((exc, order), jnp.bfloat16),
                pltpu.VMEM((FACES, exc, face), jnp.float32),
                pltpu.VMEM((slots, FACES, exc, face), jnp.bfloat16),
                pltpu.VMEM((slots, FACES, exc, face), jnp.bfloat16),
                pltpu.SemaphoreType.DMA((FACES,)),
                pltpu.SemaphoreType.DMA,
                pltpu.SemaphoreType.DMA((slots, FACES, groups)),
                pltpu.SemaphoreType.DMA((slots, FACES, groups)),
            ],
            compiler_params=pltpu.CompilerParams(
                collective_id=0, has_side_effects=True, vmem_limit_bytes=60 * 1024 * 1024
            ),
        )(square, excite, gain)
        return outgoing[None, None, None]

    placed = (
        P("row", "col", "height", None, None),
        P("row", "col", "height", None, None),
        P("row", "col", "height", None),
    )
    return jax.shard_map(
        shards,
        mesh=mesh,
        in_specs=placed,
        out_specs=P("row", "col", "height", None, None),
        check_vma=False,
    )
```

```python
import functools

import jax
import jax.numpy as jnp
from jax import lax
from jax.experimental import pallas as pl
from jax.experimental.pallas import tpu as pltpu
from jax.sharding import PartitionSpec as P

ITERS = 8
FACES = 6
AXES = ("row", "col", "height")
MESH = pl.DeviceIdType.MESH
GROUPS = ((0, 32), (32, 16))
STAGES = ((0, 2), (2, 6))
BATCHES = ((2, 3), (4, 5), (0, 1))
SEND_ORDER = sum(BATCHES, ())


def kernel(sizes, face, z_hbm, src_hbm, gain_ref, out,
           z, src, acc, zero, send, recv, z_sem, src_sem, send_sem, recv_sem):
    pos = [lax.axis_index(name) for name in AXES]

    def neighbour(f):
        axis, up = f // 2, f % 2
        n = sizes[axis]
        ids = list(pos)
        ids[axis] = lax.rem(pos[axis] + (1 if up else n - 1), n)
        return tuple(ids)

    targets = [neighbour(f) for f in range(FACES)]
    exists = [
        pos[f // 2] < sizes[f // 2] - 1 if f % 2 else pos[f // 2] > 0 for f in range(FACES)
    ]

    def z_copy(f):
        return pltpu.make_async_copy(z_hbm.at[:, f * face:(f + 1) * face], z.at[f], z_sem.at[f])

    src_copy = pltpu.make_async_copy(src_hbm, src, src_sem)
    src_copy.start()
    for f in SEND_ORDER:
        z_copy(f).start()
    barrier = pltpu.get_barrier_semaphore()
    for f in range(FACES):

        @pl.when(exists[f])
        def _():
            pl.semaphore_signal(barrier, inc=1, device_id=targets[f], device_id_type=MESH)

    zero[...] = jnp.zeros_like(zero)
    gains = [gain_ref[f].astype(jnp.float32) for f in range(FACES)]

    def remote(slot, f, g):
        rows = slice(GROUPS[g][0], sum(GROUPS[g]))
        return pltpu.make_async_remote_copy(
            src_ref=send.at[slot, f, rows],
            dst_ref=recv.at[slot, f ^ 1, rows],
            send_sem=send_sem.at[f],
            recv_sem=recv_sem.at[slot, g, 0 if f < STAGES[0][1] else 1],
            device_id=targets[f],
            device_id_type=MESH,
        )

    def launch(slot, f, g):
        rows = slice(GROUPS[g][0], sum(GROUPS[g]))

        @pl.when(exists[f])
        def _():
            remote(slot, f, g).start()

        @pl.when(jnp.logical_not(exists[f]))
        def _():
            pltpu.make_async_copy(
                zero.at[rows], recv.at[slot, f, rows], recv_sem.at[slot, g, 0 if f < STAGES[0][1] else 1]
            ).start()

    def arrived(slot, g, stage):
        rows = slice(GROUPS[g][0], sum(GROUPS[g]))
        whole = recv.at[slot, slice(*STAGES[stage]), rows]
        pltpu.make_async_copy(whole, whole, recv_sem.at[slot, g, stage]).wait()

    src_copy.wait()
    for i, f in enumerate(SEND_ORDER):
        z_copy(f).wait()
        value = jnp.dot(src[...], z[f], preferred_element_type=jnp.float32)
        send[0, f] = value.astype(jnp.bfloat16)
        if i == 0:
            pl.semaphore_wait(barrier, sum(here.astype(jnp.int32) for here in exists))
        for g in range(len(GROUPS)):
            launch(0, f, g)

    def driven(slot, g, stage):
        rows = slice(GROUPS[g][0], sum(GROUPS[g]))
        arrived(slot, g, stage)
        return jnp.concatenate(
            [
                (
                    recv[slot, f, rows].astype(jnp.float32) * gains[f]
                    + src[rows, f * face:(f + 1) * face].astype(jnp.float32)
                ).astype(jnp.bfloat16)
                for f in range(*STAGES[stage])
            ],
            axis=1,
        )

    def accept(slot, g, finish):
        rows = slice(GROUPS[g][0], sum(GROUPS[g]))
        first, second = (slice(lo * face, hi * face) for lo, hi in STAGES)
        part = driven(slot, g, 0)
        for f in SEND_ORDER:
            acc[f, rows] = jnp.dot(part, z[f, first], preferred_element_type=jnp.float32)
        rest = driven(slot, g, 1)
        for batch in BATCHES:
            values = [
                (acc[f, rows] + jnp.dot(rest, z[f, second], preferred_element_type=jnp.float32)).astype(jnp.bfloat16)
                for f in batch
            ]
            finish(rows, batch, values)

    def step(iteration, carry):
        for g in range(len(GROUPS)):

            def finish(rows, batch, values):
                for f, value in zip(batch, values):
                    send[iteration, f, rows] = value
                for f in batch:
                    launch(iteration, f, g)

            accept(iteration - 1, g, finish)
        return carry

    lax.fori_loop(1, ITERS - 1, step, 0)

    def finish_last(rows, batch, values):
        for f, value in zip(batch, values):
            out[rows, f * face:(f + 1) * face] = value

    for g in range(len(GROUPS)):
        accept(ITERS - 2, g, finish_last)
    for f in range(FACES):

        @pl.when(exists[f])
        def _():
            whole = send.at[:, f]
            pltpu.make_async_copy(whole, whole, send_sem.at[f]).wait()


def solution(mesh):
    sizes = tuple(mesh.shape[name] for name in AXES)

    def shards(impedance, sources, coupling):
        square = impedance[0, 0, 0]
        excite = sources[0, 0, 0]
        gain = coupling[0, 0, 0]
        exc, order = excite.shape
        face = order // FACES
        slots = ITERS - 1
        outgoing = pl.pallas_call(
            functools.partial(kernel, sizes, face),
            out_shape=pltpu.VMEM((exc, order), jnp.bfloat16),
            in_specs=[
                pl.BlockSpec(memory_space=pl.ANY),
                pl.BlockSpec(memory_space=pl.ANY),
                pl.BlockSpec(memory_space=pltpu.SMEM),
            ],
            out_specs=pl.BlockSpec(memory_space=pltpu.VMEM),
            scratch_shapes=[
                pltpu.VMEM((FACES, order, face), jnp.bfloat16),
                pltpu.VMEM((exc, order), jnp.bfloat16),
                pltpu.VMEM((FACES, exc, face), jnp.float32),
                pltpu.VMEM((exc, face), jnp.bfloat16),
                pltpu.VMEM((slots, FACES, exc, face), jnp.bfloat16),
                pltpu.VMEM((slots, FACES, exc, face), jnp.bfloat16),
                pltpu.SemaphoreType.DMA((FACES,)),
                pltpu.SemaphoreType.DMA,
                pltpu.SemaphoreType.DMA((FACES,)),
                pltpu.SemaphoreType.DMA((slots, len(GROUPS), len(STAGES))),
            ],
            compiler_params=pltpu.CompilerParams(
                collective_id=0, has_side_effects=True, vmem_limit_bytes=60 * 1024 * 1024
            ),
        )(square, excite, gain)
        return outgoing[None, None, None]

    placed = (
        P("row", "col", "height", None, None),
        P("row", "col", "height", None, None),
        P("row", "col", "height", None),
    )
    return jax.shard_map(
        shards,
        mesh=mesh,
        in_specs=placed,
        out_specs=P("row", "col", "height", None, None),
        check_vma=False,
    )
```

```python
import functools

import jax
import jax.numpy as jnp
from jax import lax
from jax.experimental import pallas as pl
from jax.experimental.pallas import tpu as pltpu
from jax.sharding import PartitionSpec as P

ITERS = 8
FACES = 6
AXES = ("row", "col", "height")
MESH = pl.DeviceIdType.MESH
GROUPS = ((0, 16), (16, 16), (32, 16))
STAGES = ((0, 2), (2, 6))
BATCHES = ((2, 3), (4, 5), (0, 1))
SEND_ORDER = sum(BATCHES, ())


def kernel(sizes, face, z_hbm, src_hbm, gain_ref, out,
           z, src, acc, zero, send, recv, z_sem, src_sem, send_sem, recv_sem):
    pos = [lax.axis_index(name) for name in AXES]

    def neighbour(f):
        axis, up = f // 2, f % 2
        n = sizes[axis]
        ids = list(pos)
        ids[axis] = lax.rem(pos[axis] + (1 if up else n - 1), n)
        return tuple(ids)

    targets = [neighbour(f) for f in range(FACES)]
    exists = [
        pos[f // 2] < sizes[f // 2] - 1 if f % 2 else pos[f // 2] > 0 for f in range(FACES)
    ]

    def z_copy(f):
        return pltpu.make_async_copy(z_hbm.at[:, f * face:(f + 1) * face], z.at[f], z_sem.at[f])

    src_copy = pltpu.make_async_copy(src_hbm, src, src_sem)
    src_copy.start()
    for f in SEND_ORDER:
        z_copy(f).start()
    barrier = pltpu.get_barrier_semaphore()
    for f in range(FACES):

        @pl.when(exists[f])
        def _():
            pl.semaphore_signal(barrier, inc=1, device_id=targets[f], device_id_type=MESH)

    zero[...] = jnp.zeros_like(zero)
    gains = [gain_ref[f].astype(jnp.float32) for f in range(FACES)]

    def remote(slot, f, g):
        rows = slice(GROUPS[g][0], sum(GROUPS[g]))
        return pltpu.make_async_remote_copy(
            src_ref=send.at[slot, f, rows],
            dst_ref=recv.at[slot, f ^ 1, rows],
            send_sem=send_sem.at[f],
            recv_sem=recv_sem.at[slot, g, 0 if f < STAGES[0][1] else 1],
            device_id=targets[f],
            device_id_type=MESH,
        )

    def launch(slot, f, g):
        rows = slice(GROUPS[g][0], sum(GROUPS[g]))

        @pl.when(exists[f])
        def _():
            remote(slot, f, g).start()

        @pl.when(jnp.logical_not(exists[f]))
        def _():
            pltpu.make_async_copy(
                zero.at[rows], recv.at[slot, f, rows], recv_sem.at[slot, g, 0 if f < STAGES[0][1] else 1]
            ).start()

    def arrived(slot, g, stage):
        rows = slice(GROUPS[g][0], sum(GROUPS[g]))
        whole = recv.at[slot, slice(*STAGES[stage]), rows]
        pltpu.make_async_copy(whole, whole, recv_sem.at[slot, g, stage]).wait()

    src_copy.wait()
    for i, f in enumerate(SEND_ORDER):
        z_copy(f).wait()
        value = jnp.dot(src[...], z[f], preferred_element_type=jnp.float32)
        send[0, f] = value.astype(jnp.bfloat16)
        if i == 0:
            pl.semaphore_wait(barrier, sum(here.astype(jnp.int32) for here in exists))
        for g in range(len(GROUPS)):
            launch(0, f, g)

    def driven(slot, g, stage):
        rows = slice(GROUPS[g][0], sum(GROUPS[g]))
        arrived(slot, g, stage)
        return jnp.concatenate(
            [
                (
                    recv[slot, f, rows].astype(jnp.float32) * gains[f]
                    + src[rows, f * face:(f + 1) * face].astype(jnp.float32)
                ).astype(jnp.bfloat16)
                for f in range(*STAGES[stage])
            ],
            axis=1,
        )

    def accept(slot, g, finish):
        rows = slice(GROUPS[g][0], sum(GROUPS[g]))
        first, second = (slice(lo * face, hi * face) for lo, hi in STAGES)
        part = driven(slot, g, 0)
        for f in SEND_ORDER:
            acc[f, rows] = jnp.dot(part, z[f, first], preferred_element_type=jnp.float32)
        rest = driven(slot, g, 1)
        for batch in BATCHES:
            values = [
                (acc[f, rows] + jnp.dot(rest, z[f, second], preferred_element_type=jnp.float32)).astype(jnp.bfloat16)
                for f in batch
            ]
            finish(rows, batch, values)

    def step(iteration, carry):
        for g in range(len(GROUPS)):

            def finish(rows, batch, values):
                for f, value in zip(batch, values):
                    send[iteration, f, rows] = value
                for f in batch:
                    launch(iteration, f, g)

            accept(iteration - 1, g, finish)
        return carry

    lax.fori_loop(1, ITERS - 1, step, 0)

    def finish_last(rows, batch, values):
        for f, value in zip(batch, values):
            out[rows, f * face:(f + 1) * face] = value

    for g in range(len(GROUPS)):
        accept(ITERS - 2, g, finish_last)
    for f in range(FACES):

        @pl.when(exists[f])
        def _():
            whole = send.at[:, f]
            pltpu.make_async_copy(whole, whole, send_sem.at[f]).wait()


def solution(mesh):
    sizes = tuple(mesh.shape[name] for name in AXES)

    def shards(impedance, sources, coupling):
        square = impedance[0, 0, 0]
        excite = sources[0, 0, 0]
        gain = coupling[0, 0, 0]
        exc, order = excite.shape
        face = order // FACES
        slots = ITERS - 1
        outgoing = pl.pallas_call(
            functools.partial(kernel, sizes, face),
            out_shape=pltpu.VMEM((exc, order), jnp.bfloat16),
            in_specs=[
                pl.BlockSpec(memory_space=pl.ANY),
                pl.BlockSpec(memory_space=pl.ANY),
                pl.BlockSpec(memory_space=pltpu.SMEM),
            ],
            out_specs=pl.BlockSpec(memory_space=pltpu.VMEM),
            scratch_shapes=[
                pltpu.VMEM((FACES, order, face), jnp.bfloat16),
                pltpu.VMEM((exc, order), jnp.bfloat16),
                pltpu.VMEM((FACES, exc, face), jnp.float32),
                pltpu.VMEM((exc, face), jnp.bfloat16),
                pltpu.VMEM((slots, FACES, exc, face), jnp.bfloat16),
                pltpu.VMEM((slots, FACES, exc, face), jnp.bfloat16),
                pltpu.SemaphoreType.DMA((FACES,)),
                pltpu.SemaphoreType.DMA,
                pltpu.SemaphoreType.DMA((FACES,)),
                pltpu.SemaphoreType.DMA((slots, len(GROUPS), len(STAGES))),
            ],
            compiler_params=pltpu.CompilerParams(
                collective_id=0, has_side_effects=True, vmem_limit_bytes=60 * 1024 * 1024
            ),
        )(square, excite, gain)
        return outgoing[None, None, None]

    placed = (
        P("row", "col", "height", None, None),
        P("row", "col", "height", None, None),
        P("row", "col", "height", None),
    )
    return jax.shard_map(
        shards,
        mesh=mesh,
        in_specs=placed,
        out_specs=P("row", "col", "height", None, None),
        check_vma=False,
    )
```

```python
import functools

import jax
import jax.numpy as jnp
from jax import lax
from jax.experimental import pallas as pl
from jax.experimental.pallas import tpu as pltpu
from jax.sharding import PartitionSpec as P

ITERS = 8
FACES = 6
AXES = ("row", "col", "height")
MESH = pl.DeviceIdType.MESH
GROUPS = ((0, 16), (16, 16), (32, 16))
STAGES = ((0, 2), (1,))
BATCHES = ((2, 3), (4, 5, 0, 1))
SEND_ORDER = sum(BATCHES, ())


def kernel(sizes, face, z_hbm, src_hbm, gain_ref, out,
           z, src, acc, send, recv, z_sem, src_sem, send_sem, recv_sem):
    pos = [lax.axis_index(name) for name in AXES]

    def partner(f):
        axis, up = f // 2, f % 2
        n = sizes[axis]
        here = (pos[axis] < n - 1 if up else pos[axis] > 0).astype(jnp.int32)
        ids = list(pos)
        if axis == 0:
            ids[0] = lax.rem(pos[0] + (1 if up else n - 1), n)
            return tuple(ids), f ^ 1, here
        ids[axis] = pos[axis] + here * (1 if up else -1)
        ids[0] = pos[0] + (1 - here) * (1 - 2 * lax.rem(pos[0], 2))
        return tuple(ids), f + here * (-1 if up else 1), here

    partners = [partner(f) for f in range(FACES)]

    def z_copy(f):
        return pltpu.make_async_copy(z_hbm.at[:, f * face:(f + 1) * face], z.at[f], z_sem.at[f])

    src_copy = pltpu.make_async_copy(src_hbm, src, src_sem)
    src_copy.start()
    for f in SEND_ORDER:
        z_copy(f).start()
    barrier = pltpu.get_barrier_semaphore()
    for f in range(FACES):
        pl.semaphore_signal(barrier, inc=1, device_id=partners[f][0], device_id_type=MESH)
    gains = [(gain_ref[f] * partners[f][2]).astype(jnp.float32) for f in range(FACES)]

    def launch(slot, f, g):
        rows = slice(GROUPS[g][0], sum(GROUPS[g]))
        device, landing, _ = partners[f]
        pltpu.make_async_remote_copy(
            src_ref=send.at[slot, f, rows],
            dst_ref=recv.at[slot, landing, rows],
            send_sem=send_sem.at[f],
            recv_sem=recv_sem.at[slot, g, f // 2],
            device_id=device,
            device_id_type=MESH,
        ).start()

    def arrived(slot, g, axis):
        rows = slice(GROUPS[g][0], sum(GROUPS[g]))
        whole = recv.at[slot, 2 * axis:2 * axis + 2, rows]
        pltpu.make_async_copy(whole, whole, recv_sem.at[slot, g, axis]).wait()

    src_copy.wait()
    for i, f in enumerate(SEND_ORDER):
        z_copy(f).wait()
        value = jnp.dot(src[...], z[f], preferred_element_type=jnp.float32)
        send[0, f] = value.astype(jnp.bfloat16)
        if i == 0:
            pl.semaphore_wait(barrier, FACES)
        for g in range(len(GROUPS)):
            launch(0, f, g)

    def driven(slot, g, stage):
        rows = slice(GROUPS[g][0], sum(GROUPS[g]))
        for axis in STAGES[stage]:
            arrived(slot, g, axis)
        return [
            jnp.concatenate(
                [
                    (
                        recv[slot, f, rows].astype(jnp.float32) * gains[f]
                        + src[rows, f * face:(f + 1) * face].astype(jnp.float32)
                    ).astype(jnp.bfloat16)
                    for f in (2 * axis, 2 * axis + 1)
                ],
                axis=1,
            )
            for axis in STAGES[stage]
        ]

    def times(parts, stage, f):
        return sum(
            jnp.dot(part, z[f, 2 * axis * face:(2 * axis + 2) * face], preferred_element_type=jnp.float32)
            for part, axis in zip(parts, STAGES[stage])
        )

    def accept(slot, g, finish):
        rows = slice(GROUPS[g][0], sum(GROUPS[g]))
        last = len(STAGES) - 1
        for stage in range(last):
            parts = driven(slot, g, stage)
            for f in SEND_ORDER:
                total = times(parts, stage, f)
                acc[f, rows] = total if stage == 0 else acc[f, rows] + total
        parts = driven(slot, g, last)
        for batch in BATCHES:
            finish(rows, batch, [(acc[f, rows] + times(parts, last, f)).astype(jnp.bfloat16) for f in batch])

    def step(iteration, carry):
        for g in range(len(GROUPS)):

            def finish(rows, batch, values):
                for f, value in zip(batch, values):
                    send[iteration, f, rows] = value
                for f in batch:
                    launch(iteration, f, g)

            accept(iteration - 1, g, finish)
        return carry

    lax.fori_loop(1, ITERS - 1, step, 0)

    def finish_last(rows, batch, values):
        for f, value in zip(batch, values):
            out[rows, f * face:(f + 1) * face] = value

    for g in range(len(GROUPS)):
        accept(ITERS - 2, g, finish_last)
    for f in range(FACES):
        whole = send.at[:, f]
        pltpu.make_async_copy(whole, whole, send_sem.at[f]).wait()


def solution(mesh):
    sizes = tuple(mesh.shape[name] for name in AXES)

    def shards(impedance, sources, coupling):
        square = impedance[0, 0, 0]
        excite = sources[0, 0, 0]
        gain = coupling[0, 0, 0]
        exc, order = excite.shape
        face = order // FACES
        slots = ITERS - 1
        outgoing = pl.pallas_call(
            functools.partial(kernel, sizes, face),
            out_shape=pltpu.VMEM((exc, order), jnp.bfloat16),
            in_specs=[
                pl.BlockSpec(memory_space=pl.ANY),
                pl.BlockSpec(memory_space=pl.ANY),
                pl.BlockSpec(memory_space=pltpu.SMEM),
            ],
            out_specs=pl.BlockSpec(memory_space=pltpu.VMEM),
            scratch_shapes=[
                pltpu.VMEM((FACES, order, face), jnp.bfloat16),
                pltpu.VMEM((exc, order), jnp.bfloat16),
                pltpu.VMEM((FACES, exc, face), jnp.float32),
                pltpu.VMEM((slots, FACES, exc, face), jnp.bfloat16),
                pltpu.VMEM((slots, FACES, exc, face), jnp.bfloat16),
                pltpu.SemaphoreType.DMA((FACES,)),
                pltpu.SemaphoreType.DMA,
                pltpu.SemaphoreType.DMA((FACES,)),
                pltpu.SemaphoreType.DMA((slots, len(GROUPS), len(AXES))),
            ],
            compiler_params=pltpu.CompilerParams(
                collective_id=0, has_side_effects=True, vmem_limit_bytes=60 * 1024 * 1024
            ),
        )(square, excite, gain)
        return outgoing[None, None, None]

    placed = (
        P("row", "col", "height", None, None),
        P("row", "col", "height", None, None),
        P("row", "col", "height", None),
    )
    return jax.shard_map(
        shards,
        mesh=mesh,
        in_specs=placed,
        out_specs=P("row", "col", "height", None, None),
        check_vma=False,
    )
```

```python
import functools

import jax
import jax.numpy as jnp
from jax import lax
from jax.experimental import pallas as pl
from jax.experimental.pallas import tpu as pltpu
from jax.sharding import PartitionSpec as P

ITERS = 8
FACES = 6
AXES = ("row", "col", "height")
MESH = pl.DeviceIdType.MESH
ROWS = 16
STAGES = ((0, 2), (2, 6))
BATCHES = ((2, 3), (4, 5), (0, 1))
SEND_ORDER = sum(BATCHES, ())


def kernel(sizes, face, z_hbm, src_hbm, gain_ref, out,
           z, src, acc, send, recv, z_sem, src_sem, send_sem, recv_sem):
    chains = src.shape[0]
    pos = [lax.axis_index(name) for name in AXES]

    def partner(f):
        axis, up = f // 2, f % 2
        n = sizes[axis]
        here = (pos[axis] < n - 1 if up else pos[axis] > 0).astype(jnp.int32)
        ids = list(pos)
        if axis == 0:
            ids[0] = lax.rem(pos[0] + (1 if up else n - 1), n)
            return tuple(ids), f ^ 1, here
        ids[axis] = pos[axis] + here * (1 if up else -1)
        ids[0] = pos[0] + (1 - here) * (1 - 2 * lax.rem(pos[0], 2))
        return tuple(ids), f + here * (-1 if up else 1), here

    partners = [partner(f) for f in range(FACES)]

    def z_copy(f):
        return pltpu.make_async_copy(z_hbm.at[:, f * face:(f + 1) * face], z.at[f], z_sem.at[f])

    def src_copy(g):
        return pltpu.make_async_copy(src_hbm.at[g * ROWS:(g + 1) * ROWS], src.at[g], src_sem.at[g])

    for g in range(chains):
        src_copy(g).start()
    for f in SEND_ORDER:
        z_copy(f).start()
    barrier = pltpu.get_barrier_semaphore()
    for f in range(FACES):
        pl.semaphore_signal(barrier, inc=1, device_id=partners[f][0], device_id_type=MESH)
    gains = [(gain_ref[f] * partners[f][2]).astype(jnp.float32) for f in range(FACES)]

    def launch(slot, f, g):
        device, landing, _ = partners[f]
        pltpu.make_async_remote_copy(
            src_ref=send.at[slot, g, f],
            dst_ref=recv.at[slot, g, landing],
            send_sem=send_sem.at[f],
            recv_sem=recv_sem.at[slot, g, 0 if f < STAGES[0][1] else 1],
            device_id=device,
            device_id_type=MESH,
        ).start()

    for g in range(chains):
        src_copy(g).wait()
    for i, f in enumerate(SEND_ORDER):
        z_copy(f).wait()
        value = jnp.dot(src[...].reshape(chains * ROWS, -1), z[f], preferred_element_type=jnp.float32)
        for g in range(chains):
            send[0, g, f] = value[g * ROWS:(g + 1) * ROWS].astype(jnp.bfloat16)
        if i == 0:
            pl.semaphore_wait(barrier, FACES)
        for g in range(chains):
            launch(0, f, g)

    def driven(slot, g, stage):
        whole = recv.at[slot, g, slice(*STAGES[stage])]
        pltpu.make_async_copy(whole, whole, recv_sem.at[slot, g, stage]).wait()
        return jnp.concatenate(
            [
                (
                    recv[slot, g, f].astype(jnp.float32) * gains[f]
                    + src[g, :, f * face:(f + 1) * face].astype(jnp.float32)
                ).astype(jnp.bfloat16)
                for f in range(*STAGES[stage])
            ],
            axis=1,
        )

    first, second = (slice(lo * face, hi * face) for lo, hi in STAGES)

    def step(iteration, carry):
        def chain(g, carry):
            part = driven(iteration - 1, g, 0)
            for f in SEND_ORDER:
                acc[f] = jnp.dot(part, z[f, first], preferred_element_type=jnp.float32)
            rest = driven(iteration - 1, g, 1)
            for batch in BATCHES:
                for f in batch:
                    total = acc[f] + jnp.dot(rest, z[f, second], preferred_element_type=jnp.float32)
                    send[iteration, g, f] = total.astype(jnp.bfloat16)

                @pl.when(iteration < ITERS - 1)
                def _():
                    for f in batch:
                        launch(iteration, f, g)

            return carry

        return lax.fori_loop(0, chains, chain, carry)

    lax.fori_loop(1, ITERS, step, 0)

    for g in range(chains):
        for f in range(FACES):
            out[g * ROWS:(g + 1) * ROWS, f * face:(f + 1) * face] = send[ITERS - 1, g, f]
    for f in range(FACES):
        whole = send.at[0:ITERS - 1, :, f]
        pltpu.make_async_copy(whole, whole, send_sem.at[f]).wait()


def solution(mesh):
    sizes = tuple(mesh.shape[name] for name in AXES)

    def shards(impedance, sources, coupling):
        square = impedance[0, 0, 0]
        excite = sources[0, 0, 0]
        gain = coupling[0, 0, 0]
        exc, order = excite.shape
        face = order // FACES
        chains = exc // ROWS
        outgoing = pl.pallas_call(
            functools.partial(kernel, sizes, face),
            out_shape=pltpu.VMEM((exc, order), jnp.bfloat16),
            in_specs=[
                pl.BlockSpec(memory_space=pl.ANY),
                pl.BlockSpec(memory_space=pl.ANY),
                pl.BlockSpec(memory_space=pltpu.SMEM),
            ],
            out_specs=pl.BlockSpec(memory_space=pltpu.VMEM),
            scratch_shapes=[
                pltpu.VMEM((FACES, order, face), jnp.bfloat16),
                pltpu.VMEM((chains, ROWS, order), jnp.bfloat16),
                pltpu.VMEM((FACES, ROWS, face), jnp.float32),
                pltpu.VMEM((ITERS, chains, FACES, ROWS, face), jnp.bfloat16),
                pltpu.VMEM((ITERS - 1, chains, FACES, ROWS, face), jnp.bfloat16),
                pltpu.SemaphoreType.DMA((FACES,)),
                pltpu.SemaphoreType.DMA((chains,)),
                pltpu.SemaphoreType.DMA((FACES,)),
                pltpu.SemaphoreType.DMA((ITERS - 1, chains, len(STAGES))),
            ],
            compiler_params=pltpu.CompilerParams(
                collective_id=0, has_side_effects=True, vmem_limit_bytes=60 * 1024 * 1024
            ),
        )(square, excite, gain)
        return outgoing[None, None, None]

    placed = (
        P("row", "col", "height", None, None),
        P("row", "col", "height", None, None),
        P("row", "col", "height", None),
    )
    return jax.shard_map(
        shards,
        mesh=mesh,
        in_specs=placed,
        out_specs=P("row", "col", "height", None, None),
        check_vma=False,
    )
```

```python
import functools

import jax
import jax.numpy as jnp
from jax import lax
from jax.experimental import pallas as pl
from jax.experimental.pallas import tpu as pltpu
from jax.sharding import PartitionSpec as P

ITERS = 8
FACES = 6
AXES = ("row", "col", "height")
MESH = pl.DeviceIdType.MESH
ROWS = 16
STAGES = ((0, 2), (2, 6))
BATCHES = ((2, 3), (4, 5), (0, 1))
SEND_ORDER = sum(BATCHES, ())


def kernel(sizes, face, z_hbm, src_hbm, gain_ref, out,
           z, src, acc, send, recv, z_sem, src_sem, send_sem, recv_sem):
    chains = src.shape[0]
    pos = [lax.axis_index(name) for name in AXES]

    def partner(f):
        axis, up = f // 2, f % 2
        n = sizes[axis]
        here = (pos[axis] < n - 1 if up else pos[axis] > 0).astype(jnp.int32)
        ids = list(pos)
        if axis == 0:
            ids[0] = lax.rem(pos[0] + (1 if up else n - 1), n)
            return tuple(ids), f ^ 1, here
        ids[axis] = pos[axis] + here * (1 if up else -1)
        ids[0] = pos[0] + (1 - here) * (1 - 2 * lax.rem(pos[0], 2))
        return tuple(ids), f + here * (-1 if up else 1), here

    partners = [partner(f) for f in range(FACES)]

    def z_copy(f):
        return pltpu.make_async_copy(z_hbm.at[:, f * face:(f + 1) * face], z.at[f], z_sem.at[f])

    def src_copy(g):
        return pltpu.make_async_copy(src_hbm.at[g * ROWS:(g + 1) * ROWS], src.at[g], src_sem.at[g])

    for g in range(chains):
        src_copy(g).start()
    for f in SEND_ORDER:
        z_copy(f).start()
    barrier = pltpu.get_barrier_semaphore()
    for f in range(FACES):
        pl.semaphore_signal(barrier, inc=1, device_id=partners[f][0], device_id_type=MESH)
    gains = [(gain_ref[f] * partners[f][2]).astype(jnp.float32) for f in range(FACES)]

    swap = lax.rem(pos[0], 2)

    def launch(slot, f, g):
        (device, landing, _), (other, other_landing, _) = partners[f], partners[f ^ 1]
        device = tuple(a + swap * (b - a) for a, b in zip(device, other))
        landing = landing + swap * (other_landing - landing)
        stage = 0 if f < STAGES[0][1] else 1
        f = f + swap * (1 - 2 * (f % 2))
        pltpu.make_async_remote_copy(
            src_ref=send.at[slot, g, f],
            dst_ref=recv.at[slot, g, landing],
            send_sem=send_sem.at[f],
            recv_sem=recv_sem.at[slot, g, stage],
            device_id=device,
            device_id_type=MESH,
        ).start()

    for g in range(chains):
        src_copy(g).wait()
    for i, batch in enumerate(BATCHES):
        for f in batch:
            z_copy(f).wait()
            value = jnp.dot(src[...].reshape(chains * ROWS, -1), z[f], preferred_element_type=jnp.float32)
            for g in range(chains):
                send[0, g, f] = value[g * ROWS:(g + 1) * ROWS].astype(jnp.bfloat16)
        if i == 0:
            pl.semaphore_wait(barrier, FACES)
        for g in range(chains):
            for f in batch:
                launch(0, f, g)

    def driven(slot, g, stage):
        whole = recv.at[slot, g, slice(*STAGES[stage])]
        pltpu.make_async_copy(whole, whole, recv_sem.at[slot, g, stage]).wait()
        return jnp.concatenate(
            [
                (
                    recv[slot, g, f].astype(jnp.float32) * gains[f]
                    + src[g, :, f * face:(f + 1) * face].astype(jnp.float32)
                ).astype(jnp.bfloat16)
                for f in range(*STAGES[stage])
            ],
            axis=1,
        )

    first, second = (slice(lo * face, hi * face) for lo, hi in STAGES)

    def step(iteration, carry):
        def chain(g, carry):
            part = driven(iteration - 1, g, 0)
            for f in SEND_ORDER:
                acc[f] = jnp.dot(part, z[f, first], preferred_element_type=jnp.float32)
            rest = driven(iteration - 1, g, 1)
            for batch in BATCHES:
                for f in batch:
                    total = acc[f] + jnp.dot(rest, z[f, second], preferred_element_type=jnp.float32)
                    send[iteration, g, f] = total.astype(jnp.bfloat16)

                @pl.when(iteration < ITERS - 1)
                def _():
                    for f in batch:
                        launch(iteration, f, g)

            return carry

        return lax.fori_loop(0, chains, chain, carry)

    lax.fori_loop(1, ITERS, step, 0)

    for g in range(chains):
        for f in range(FACES):
            out[g * ROWS:(g + 1) * ROWS, f * face:(f + 1) * face] = send[ITERS - 1, g, f]
    for f in range(FACES):
        whole = send.at[0:ITERS - 1, :, f]
        pltpu.make_async_copy(whole, whole, send_sem.at[f]).wait()


def solution(mesh):
    sizes = tuple(mesh.shape[name] for name in AXES)

    def shards(impedance, sources, coupling):
        square = impedance[0, 0, 0]
        excite = sources[0, 0, 0]
        gain = coupling[0, 0, 0]
        exc, order = excite.shape
        face = order // FACES
        chains = exc // ROWS
        outgoing = pl.pallas_call(
            functools.partial(kernel, sizes, face),
            out_shape=pltpu.VMEM((exc, order), jnp.bfloat16),
            in_specs=[
                pl.BlockSpec(memory_space=pl.ANY),
                pl.BlockSpec(memory_space=pl.ANY),
                pl.BlockSpec(memory_space=pltpu.SMEM),
            ],
            out_specs=pl.BlockSpec(memory_space=pltpu.VMEM),
            scratch_shapes=[
                pltpu.VMEM((FACES, order, face), jnp.bfloat16),
                pltpu.VMEM((chains, ROWS, order), jnp.bfloat16),
                pltpu.VMEM((FACES, ROWS, face), jnp.float32),
                pltpu.VMEM((ITERS, chains, FACES, ROWS, face), jnp.bfloat16),
                pltpu.VMEM((ITERS - 1, chains, FACES, ROWS, face), jnp.bfloat16),
                pltpu.SemaphoreType.DMA((FACES,)),
                pltpu.SemaphoreType.DMA((chains,)),
                pltpu.SemaphoreType.DMA((FACES,)),
                pltpu.SemaphoreType.DMA((ITERS - 1, chains, len(STAGES))),
            ],
            compiler_params=pltpu.CompilerParams(
                collective_id=0, has_side_effects=True, vmem_limit_bytes=60 * 1024 * 1024
            ),
        )(square, excite, gain)
        return outgoing[None, None, None]

    placed = (
        P("row", "col", "height", None, None),
        P("row", "col", "height", None, None),
        P("row", "col", "height", None),
    )
    return jax.shard_map(
        shards,
        mesh=mesh,
        in_specs=placed,
        out_specs=P("row", "col", "height", None, None),
        check_vma=False,
    )
```

```python
import functools

import jax
import jax.numpy as jnp
from jax import lax
from jax.experimental import pallas as pl
from jax.experimental.pallas import tpu as pltpu
from jax.sharding import PartitionSpec as P

ITERS = 8
FACES = 6
AXES = ("row", "col", "height")
MESH = pl.DeviceIdType.MESH
ROWS = 16
STAGES = ((0, 2), (2, 6))
BATCHES = ((2, 3), (4, 5), (0, 1))
SEND_ORDER = sum(BATCHES, ())


def kernel(sizes, face, z_hbm, src_hbm, gain_hbm, out,
           gain_ref, z, src, acc, send, recv, gain_sem, z_sem, src_sem, send_sem, recv_sem):
    chains = src.shape[0]
    pos = [lax.axis_index(name) for name in AXES]

    def partner(f):
        axis, up = f // 2, f % 2
        n = sizes[axis]
        here = (pos[axis] < n - 1 if up else pos[axis] > 0).astype(jnp.int32)
        ids = list(pos)
        if axis == 0:
            ids[0] = lax.rem(pos[0] + (1 if up else n - 1), n)
            return tuple(ids), f ^ 1, here
        ids[axis] = pos[axis] + here * (1 if up else -1)
        ids[0] = pos[0] + (1 - here) * (1 - 2 * lax.rem(pos[0], 2))
        return tuple(ids), f + here * (-1 if up else 1), here

    partners = [partner(f) for f in range(FACES)]

    def z_copy(f):
        return pltpu.make_async_copy(z_hbm.at[:, f * face:(f + 1) * face], z.at[f], z_sem.at[f])

    def src_copy(g):
        return pltpu.make_async_copy(src_hbm.at[g * ROWS:(g + 1) * ROWS], src.at[g], src_sem.at[g])

    barrier = pltpu.get_barrier_semaphore()
    for f in range(FACES):
        pl.semaphore_signal(barrier, inc=1, device_id=partners[f][0], device_id_type=MESH)
    for g in range(chains):
        src_copy(g).start()
    for f in SEND_ORDER:
        z_copy(f).start()
    gain_copy = pltpu.make_async_copy(gain_hbm, gain_ref, gain_sem)
    gain_copy.start()

    def launch(slot, f, g):
        device, landing, _ = partners[f]
        pltpu.make_async_remote_copy(
            src_ref=send.at[slot, g, f],
            dst_ref=recv.at[slot, g, landing],
            send_sem=send_sem.at[f],
            recv_sem=recv_sem.at[slot, g, 0 if f < STAGES[0][1] else 1],
            device_id=device,
            device_id_type=MESH,
        ).start()

    for g in range(chains):
        src_copy(g).wait()
    for i, f in enumerate(SEND_ORDER):
        z_copy(f).wait()
        value = jnp.dot(src[...].reshape(chains * ROWS, -1), z[f], preferred_element_type=jnp.float32)
        for g in range(chains):
            send[0, g, f] = value[g * ROWS:(g + 1) * ROWS].astype(jnp.bfloat16)
        if i == 0:
            pl.semaphore_wait(barrier, FACES)
        for g in range(chains):
            launch(0, f, g)

    gain_copy.wait()
    gains = [(gain_ref[f] * partners[f][2]).astype(jnp.float32) for f in range(FACES)]

    def driven(slot, g, stage):
        whole = recv.at[slot, g, slice(*STAGES[stage])]
        pltpu.make_async_copy(whole, whole, recv_sem.at[slot, g, stage]).wait()
        return jnp.concatenate(
            [
                (
                    recv[slot, g, f].astype(jnp.float32) * gains[f]
                    + src[g, :, f * face:(f + 1) * face].astype(jnp.float32)
                ).astype(jnp.bfloat16)
                for f in range(*STAGES[stage])
            ],
            axis=1,
        )

    first, second = (slice(lo * face, hi * face) for lo, hi in STAGES)

    def step(iteration, carry):
        def chain(g, carry):
            part = driven(iteration - 1, g, 0)
            for f in SEND_ORDER:
                acc[f] = jnp.dot(part, z[f, first], preferred_element_type=jnp.float32)
            rest = driven(iteration - 1, g, 1)
            for batch in BATCHES:
                for f in batch:
                    total = acc[f] + jnp.dot(rest, z[f, second], preferred_element_type=jnp.float32)
                    send[iteration, g, f] = total.astype(jnp.bfloat16)

                @pl.when(iteration < ITERS - 1)
                def _():
                    for f in batch:
                        launch(iteration, f, g)

            return carry

        return lax.fori_loop(0, chains, chain, carry)

    lax.fori_loop(1, ITERS, step, 0)

    for g in range(chains):
        for f in range(FACES):
            out[g * ROWS:(g + 1) * ROWS, f * face:(f + 1) * face] = send[ITERS - 1, g, f]
    for f in range(FACES):
        whole = send.at[0:ITERS - 1, :, f]
        pltpu.make_async_copy(whole, whole, send_sem.at[f]).wait()


def solution(mesh):
    sizes = tuple(mesh.shape[name] for name in AXES)

    def shards(impedance, sources, coupling):
        square = impedance[0, 0, 0]
        excite = sources[0, 0, 0]
        gain = coupling[0, 0, 0]
        exc, order = excite.shape
        face = order // FACES
        chains = exc // ROWS
        outgoing = pl.pallas_call(
            functools.partial(kernel, sizes, face),
            out_shape=pltpu.VMEM((exc, order), jnp.bfloat16),
            in_specs=[
                pl.BlockSpec(memory_space=pl.ANY),
                pl.BlockSpec(memory_space=pl.ANY),
                pl.BlockSpec(memory_space=pl.ANY),
            ],
            out_specs=pl.BlockSpec(memory_space=pltpu.VMEM),
            scratch_shapes=[
                pltpu.SMEM((FACES,), jnp.int32),
                pltpu.VMEM((FACES, order, face), jnp.bfloat16),
                pltpu.VMEM((chains, ROWS, order), jnp.bfloat16),
                pltpu.VMEM((FACES, ROWS, face), jnp.float32),
                pltpu.VMEM((ITERS, chains, FACES, ROWS, face), jnp.bfloat16),
                pltpu.VMEM((ITERS - 1, chains, FACES, ROWS, face), jnp.bfloat16),
                pltpu.SemaphoreType.DMA,
                pltpu.SemaphoreType.DMA((FACES,)),
                pltpu.SemaphoreType.DMA((chains,)),
                pltpu.SemaphoreType.DMA((FACES,)),
                pltpu.SemaphoreType.DMA((ITERS - 1, chains, len(STAGES))),
            ],
            compiler_params=pltpu.CompilerParams(
                collective_id=0, has_side_effects=True, vmem_limit_bytes=60 * 1024 * 1024
            ),
        )(square, excite, gain)
        return outgoing[None, None, None]

    placed = (
        P("row", "col", "height", None, None),
        P("row", "col", "height", None, None),
        P("row", "col", "height", None),
    )
    return jax.shard_map(
        shards,
        mesh=mesh,
        in_specs=placed,
        out_specs=P("row", "col", "height", None, None),
        check_vma=False,
    )
```

```python
import functools

import jax
import jax.numpy as jnp
from jax import lax
from jax.experimental import pallas as pl
from jax.experimental.pallas import tpu as pltpu
from jax.sharding import PartitionSpec as P

ITERS = 8
FACES = 6
AXES = ("row", "col", "height")
MESH = pl.DeviceIdType.MESH
ROWS = 16
STAGES = ((0, 2), (2, 6))
BATCHES = ((2, 3), (4, 5), (0, 1))
SEND_ORDER = sum(BATCHES, ())
LOADS = 3


def kernel(sizes, face, z_hbm, src_hbm, gain_hbm, out,
           gain_ref, z, src, acc, send, recv, gain_sem, z_sem, src_sem, send_sem, recv_sem):
    chains = src.shape[0]
    pos = [lax.axis_index(name) for name in AXES]

    def partner(f):
        axis, up = f // 2, f % 2
        n = sizes[axis]
        here = (pos[axis] < n - 1 if up else pos[axis] > 0).astype(jnp.int32)
        ids = list(pos)
        if axis == 0:
            ids[0] = lax.rem(pos[0] + (1 if up else n - 1), n)
            return tuple(ids), f ^ 1, here
        ids[axis] = pos[axis] + here * (1 if up else -1)
        ids[0] = pos[0] + (1 - here) * (1 - 2 * lax.rem(pos[0], 2))
        return tuple(ids), f + here * (-1 if up else 1), here

    partners = [partner(f) for f in range(FACES)]

    def z_copy(f):
        return pltpu.make_async_copy(z_hbm.at[:, f * face:(f + 1) * face], z.at[f], z_sem.at[f])

    def src_copy(g):
        return pltpu.make_async_copy(src_hbm.at[g * ROWS:(g + 1) * ROWS], src.at[g], src_sem.at[g])

    barrier = pltpu.get_barrier_semaphore()
    for f in range(FACES):
        pl.semaphore_signal(barrier, inc=1, device_id=partners[f][0], device_id_type=MESH)
    for g in range(chains):
        src_copy(g).start()
    for f in SEND_ORDER[:LOADS]:
        z_copy(f).start()
    gain_copy = pltpu.make_async_copy(gain_hbm, gain_ref, gain_sem)
    gain_copy.start()

    def launch(slot, f, g):
        device, landing, _ = partners[f]
        pltpu.make_async_remote_copy(
            src_ref=send.at[slot, g, f],
            dst_ref=recv.at[slot, g, landing],
            send_sem=send_sem.at[f],
            recv_sem=recv_sem.at[slot, g, 0 if f < STAGES[0][1] else 1],
            device_id=device,
            device_id_type=MESH,
        ).start()

    for g in range(chains):
        src_copy(g).wait()
    for i, f in enumerate(SEND_ORDER):
        z_copy(f).wait()
        if i + LOADS < FACES:
            z_copy(SEND_ORDER[i + LOADS]).start()
        value = jnp.dot(src[...].reshape(chains * ROWS, -1), z[f], preferred_element_type=jnp.float32)
        for g in range(chains):
            send[0, g, f] = value[g * ROWS:(g + 1) * ROWS].astype(jnp.bfloat16)
        if i == 0:
            pl.semaphore_wait(barrier, FACES)
        for g in range(chains):
            launch(0, f, g)

    gain_copy.wait()
    gains = [(gain_ref[f] * partners[f][2]).astype(jnp.float32) for f in range(FACES)]

    def driven(slot, g, stage):
        whole = recv.at[slot, g, slice(*STAGES[stage])]
        pltpu.make_async_copy(whole, whole, recv_sem.at[slot, g, stage]).wait()
        return jnp.concatenate(
            [
                (
                    recv[slot, g, f].astype(jnp.float32) * gains[f]
                    + src[g, :, f * face:(f + 1) * face].astype(jnp.float32)
                ).astype(jnp.bfloat16)
                for f in range(*STAGES[stage])
            ],
            axis=1,
        )

    first, second = (slice(lo * face, hi * face) for lo, hi in STAGES)

    def step(iteration, carry):
        def chain(g, carry):
            part = driven(iteration - 1, g, 0)
            for f in SEND_ORDER:
                acc[f] = jnp.dot(part, z[f, first], preferred_element_type=jnp.float32)
            rest = driven(iteration - 1, g, 1)
            for batch in BATCHES:
                for f in batch:
                    total = acc[f] + jnp.dot(rest, z[f, second], preferred_element_type=jnp.float32)
                    send[iteration, g, f] = total.astype(jnp.bfloat16)

                @pl.when(iteration < ITERS - 1)
                def _():
                    for f in batch:
                        launch(iteration, f, g)

            return carry

        return lax.fori_loop(0, chains, chain, carry)

    lax.fori_loop(1, ITERS, step, 0)

    for g in range(chains):
        for f in range(FACES):
            out[g * ROWS:(g + 1) * ROWS, f * face:(f + 1) * face] = send[ITERS - 1, g, f]
    for f in range(FACES):
        whole = send.at[0:ITERS - 1, :, f]
        pltpu.make_async_copy(whole, whole, send_sem.at[f]).wait()


def solution(mesh):
    sizes = tuple(mesh.shape[name] for name in AXES)

    def shards(impedance, sources, coupling):
        square = impedance[0, 0, 0]
        excite = sources[0, 0, 0]
        gain = coupling[0, 0, 0]
        exc, order = excite.shape
        face = order // FACES
        chains = exc // ROWS
        outgoing = pl.pallas_call(
            functools.partial(kernel, sizes, face),
            out_shape=pltpu.VMEM((exc, order), jnp.bfloat16),
            in_specs=[
                pl.BlockSpec(memory_space=pl.ANY),
                pl.BlockSpec(memory_space=pl.ANY),
                pl.BlockSpec(memory_space=pl.ANY),
            ],
            out_specs=pl.BlockSpec(memory_space=pltpu.VMEM),
            scratch_shapes=[
                pltpu.SMEM((FACES,), jnp.int32),
                pltpu.VMEM((FACES, order, face), jnp.bfloat16),
                pltpu.VMEM((chains, ROWS, order), jnp.bfloat16),
                pltpu.VMEM((FACES, ROWS, face), jnp.float32),
                pltpu.VMEM((ITERS, chains, FACES, ROWS, face), jnp.bfloat16),
                pltpu.VMEM((ITERS - 1, chains, FACES, ROWS, face), jnp.bfloat16),
                pltpu.SemaphoreType.DMA,
                pltpu.SemaphoreType.DMA((FACES,)),
                pltpu.SemaphoreType.DMA((chains,)),
                pltpu.SemaphoreType.DMA((FACES,)),
                pltpu.SemaphoreType.DMA((ITERS - 1, chains, len(STAGES))),
            ],
            compiler_params=pltpu.CompilerParams(
                collective_id=0, has_side_effects=True, vmem_limit_bytes=60 * 1024 * 1024
            ),
        )(square, excite, gain)
        return outgoing[None, None, None]

    placed = (
        P("row", "col", "height", None, None),
        P("row", "col", "height", None, None),
        P("row", "col", "height", None),
    )
    return jax.shard_map(
        shards,
        mesh=mesh,
        in_specs=placed,
        out_specs=P("row", "col", "height", None, None),
        check_vma=False,
    )
```

```python
import functools

import jax
import jax.numpy as jnp
from jax import lax
from jax.experimental import pallas as pl
from jax.experimental.pallas import tpu as pltpu
from jax.sharding import PartitionSpec as P

ITERS = 8
FACES = 6
AXES = ("row", "col", "height")
MESH = pl.DeviceIdType.MESH
ROWS = 16
STAGES = ((0, 2), (2, 6))
BATCHES = ((4, 5), (2, 3), (0, 1))
SEND_ORDER = sum(BATCHES, ())
LOADS = 2


def kernel(sizes, face, z_hbm, src_hbm, gain_hbm, out,
           gain_ref, z, src, acc, send, recv, gain_sem, z_sem, src_sem, send_sem, recv_sem):
    chains = src.shape[0]
    pos = [lax.axis_index(name) for name in AXES]

    def partner(f):
        axis, up = f // 2, f % 2
        n = sizes[axis]
        here = (pos[axis] < n - 1 if up else pos[axis] > 0).astype(jnp.int32)
        ids = list(pos)
        if axis == 0:
            ids[0] = lax.rem(pos[0] + (1 if up else n - 1), n)
            return tuple(ids), f ^ 1, here
        ids[axis] = pos[axis] + here * (1 if up else -1)
        ids[0] = pos[0] + (1 - here) * (1 - 2 * lax.rem(pos[0], 2))
        return tuple(ids), f + here * (-1 if up else 1), here

    partners = [partner(f) for f in range(FACES)]

    def z_copy(f):
        return pltpu.make_async_copy(z_hbm.at[:, f * face:(f + 1) * face], z.at[f], z_sem.at[f])

    def src_copy(g):
        return pltpu.make_async_copy(src_hbm.at[g * ROWS:(g + 1) * ROWS], src.at[g], src_sem.at[g])

    barrier = pltpu.get_barrier_semaphore()
    for f in range(FACES):
        pl.semaphore_signal(barrier, inc=1, device_id=partners[f][0], device_id_type=MESH)
    for g in range(chains):
        src_copy(g).start()
    for f in SEND_ORDER[:LOADS]:
        z_copy(f).start()
    gain_copy = pltpu.make_async_copy(gain_hbm, gain_ref, gain_sem)
    gain_copy.start()

    def launch(slot, f, g):
        device, landing, _ = partners[f]
        pltpu.make_async_remote_copy(
            src_ref=send.at[slot, g, f],
            dst_ref=recv.at[slot, g, landing],
            send_sem=send_sem.at[f],
            recv_sem=recv_sem.at[slot, g, 0 if f < STAGES[0][1] else 1],
            device_id=device,
            device_id_type=MESH,
        ).start()

    for g in range(chains):
        src_copy(g).wait()
    for i, f in enumerate(SEND_ORDER):
        z_copy(f).wait()
        if i + LOADS < FACES:
            z_copy(SEND_ORDER[i + LOADS]).start()
        value = jnp.dot(src[...].reshape(chains * ROWS, -1), z[f], preferred_element_type=jnp.float32)
        for g in range(chains):
            send[0, g, f] = value[g * ROWS:(g + 1) * ROWS].astype(jnp.bfloat16)
        if i == 0:
            pl.semaphore_wait(barrier, FACES)
        for g in range(chains):
            launch(0, f, g)

    gain_copy.wait()
    gains = [(gain_ref[f] * partners[f][2]).astype(jnp.float32) for f in range(FACES)]

    def driven(slot, g, stage):
        whole = recv.at[slot, g, slice(*STAGES[stage])]
        pltpu.make_async_copy(whole, whole, recv_sem.at[slot, g, stage]).wait()
        return jnp.concatenate(
            [
                (
                    recv[slot, g, f].astype(jnp.float32) * gains[f]
                    + src[g, :, f * face:(f + 1) * face].astype(jnp.float32)
                ).astype(jnp.bfloat16)
                for f in range(*STAGES[stage])
            ],
            axis=1,
        )

    first, second = (slice(lo * face, hi * face) for lo, hi in STAGES)

    def step(iteration, carry):
        def chain(g, carry):
            part = driven(iteration - 1, g, 0)
            for f in SEND_ORDER:
                acc[f] = jnp.dot(part, z[f, first], preferred_element_type=jnp.float32)
            rest = driven(iteration - 1, g, 1)
            for batch in BATCHES:
                for f in batch:
                    total = acc[f] + jnp.dot(rest, z[f, second], preferred_element_type=jnp.float32)
                    send[iteration, g, f] = total.astype(jnp.bfloat16)

                @pl.when(iteration < ITERS - 1)
                def _():
                    for f in batch:
                        launch(iteration, f, g)

            return carry

        return lax.fori_loop(0, chains, chain, carry)

    lax.fori_loop(1, ITERS, step, 0)

    for g in range(chains):
        for f in range(FACES):
            out[g * ROWS:(g + 1) * ROWS, f * face:(f + 1) * face] = send[ITERS - 1, g, f]
    for f in range(FACES):
        whole = send.at[0:ITERS - 1, :, f]
        pltpu.make_async_copy(whole, whole, send_sem.at[f]).wait()


def solution(mesh):
    sizes = tuple(mesh.shape[name] for name in AXES)

    def shards(impedance, sources, coupling):
        square = impedance[0, 0, 0]
        excite = sources[0, 0, 0]
        gain = coupling[0, 0, 0]
        exc, order = excite.shape
        face = order // FACES
        chains = exc // ROWS
        outgoing = pl.pallas_call(
            functools.partial(kernel, sizes, face),
            out_shape=pltpu.VMEM((exc, order), jnp.bfloat16),
            in_specs=[
                pl.BlockSpec(memory_space=pl.ANY),
                pl.BlockSpec(memory_space=pl.ANY),
                pl.BlockSpec(memory_space=pl.ANY),
            ],
            out_specs=pl.BlockSpec(memory_space=pltpu.VMEM),
            scratch_shapes=[
                pltpu.SMEM((FACES,), jnp.int32),
                pltpu.VMEM((FACES, order, face), jnp.bfloat16),
                pltpu.VMEM((chains, ROWS, order), jnp.bfloat16),
                pltpu.VMEM((FACES, ROWS, face), jnp.float32),
                pltpu.VMEM((ITERS, chains, FACES, ROWS, face), jnp.bfloat16),
                pltpu.VMEM((ITERS - 1, chains, FACES, ROWS, face), jnp.bfloat16),
                pltpu.SemaphoreType.DMA,
                pltpu.SemaphoreType.DMA((FACES,)),
                pltpu.SemaphoreType.DMA((chains,)),
                pltpu.SemaphoreType.DMA((FACES,)),
                pltpu.SemaphoreType.DMA((ITERS - 1, chains, len(STAGES))),
            ],
            compiler_params=pltpu.CompilerParams(
                collective_id=0, has_side_effects=True, vmem_limit_bytes=60 * 1024 * 1024
            ),
        )(square, excite, gain)
        return outgoing[None, None, None]

    placed = (
        P("row", "col", "height", None, None),
        P("row", "col", "height", None, None),
        P("row", "col", "height", None),
    )
    return jax.shard_map(
        shards,
        mesh=mesh,
        in_specs=placed,
        out_specs=P("row", "col", "height", None, None),
        check_vma=False,
    )
```
